512 devices in a mesh: chan: 64 (over y, x, z_hi, core), tm: 8 (over z_lo).
Axes of the slice: x: 4, y: 4, z: 16 (z_hi: 2, z_lo: 8; z = z_hi * 8 + z_lo), core: 2. Of those that a mesh axis runs over, the one named last changes fastest.
Arguments:
- raw: bfloat16 [8192, 32, 3072], P('chan', 'tm')
- alive: int32 [8192], P('chan'), may hold values 0 or 1
- use: int32 [32], P('tm'), may hold values 0 or 1
Outputs:
- stack: bfloat16 [8192, 128, 256], P(('chan', 'tm'))
The draws below stay inside these ranges and needn't reach their ends.
All inputs are finite; a program needn't handle non-finite values. No bound on the sum of `alive` or of `use` on one device may be relied on, other than what follows from the above.
Results may differ from the reference program's by a relative error of at most 0.0067.
Values may be sent and summed in bfloat16 or wider, within the bound.
No kernel may reach another device: no remote copies, remote signals or barrier semaphores. Data moves between devices by JAX's collectives and lax.ppermute only.
A program may use at most 128 MiB of HBM per device.

```python
import math
import jax
import jax.numpy as jnp
from jax import lax

CH_DEV = 128
NSAMP = 3072
BINS = 128
OFFS = 128
CHANNELS = 8192
SEGMENTS = 32


def draw_raw(key, part):
    key = jax.random.fold_in(key, 11)
    key_noise, key_common, key_weight, key_amp = jax.random.split(key, 4)
    noise = jax.random.normal(key_noise, (CHANNELS, SEGMENTS, NSAMP), jnp.float32)
    weight = jax.random.uniform(key_weight, (CHANNELS, 1, 1), jnp.float32, 0.2, 0.8)
    growth = 2.0
    common = jax.random.normal(key_common, (1, SEGMENTS, NSAMP), jnp.float32)
    amp = jnp.exp(jax.random.uniform(key_amp, (CHANNELS, SEGMENTS, 1), jnp.float32, 0.0, math.log(10.0)))
    position = jnp.arange(SEGMENTS, dtype=jnp.float32) / max(SEGMENTS - 1, 1)
    rising = (1.0 + growth * position)[None, :, None]
    return (amp * rising * (noise + weight * common)).astype(jnp.bfloat16)


def with_ends(drawn, stream_key, smallest, top_value):
    dims = drawn.shape
    spot = [jax.random.randint(jax.random.fold_in(stream_key, axis), (), 0, dims[axis]) for axis in range(len(dims))]
    drawn = drawn.at[tuple(spot)].set(smallest)
    longest = dims.index(max(dims))
    spot[longest] = (spot[longest] + 1) % dims[longest]
    return drawn.at[tuple(spot)].set(top_value)


def setup_inputs(seed: int = 0) -> dict:
    splits = jax.random.split(jax.random.key(seed), 4)
    raw = draw_raw(jax.random.fold_in(splits[3], 71), 0)
    alive = with_ends((jax.random.randint(splits[1], (CHANNELS,), 0, 8) < 7).astype(jnp.int32), jax.random.fold_in(splits[1], 1), 0, 1)
    use = with_ends((jax.random.randint(splits[2], (SEGMENTS,), 0, 4) < 3).astype(jnp.int32), jax.random.fold_in(splits[2], 1), 0, 1)
    return {"raw": raw, "alive": alive, "use": use}


def make_basis(nsamp, bins):
    times = jnp.arange(nsamp, dtype=jnp.int32)[:, None]
    freqs = jnp.arange(1, bins + 1, dtype=jnp.int32)[None, :]
    phase = (times * freqs % nsamp).astype(jnp.float32) * (2.0 * math.pi / nsamp)
    scale = 1.0 / math.sqrt(nsamp)
    return (jnp.concatenate([jnp.cos(phase), -jnp.sin(phase)], axis=1) * scale).astype(jnp.bfloat16)

def band_rows(values, rows, keep):
    width = values.shape[1]
    depth = values.shape[2]
    flat = values.reshape(rows * width, depth)
    flat = jnp.pad(flat, ((0, rows), (0, 0)))
    return flat.reshape(rows, width + 1, depth)[:, :keep]

def reference(raw, alive, use):
    basis = make_basis(NSAMP, BINS)
    blocks = CHANNELS // CH_DEV
    use_f = use.astype(jnp.float32)

    def whiten(args):
        block, flags = args
        signal = block.astype(jnp.float32)
        meansq = lax.optimization_barrier(jnp.mean(signal * signal, axis=-1, keepdims=True))
        normed = (signal * lax.rsqrt(meansq + 1e-06)).astype(jnp.bfloat16)
        spec = jnp.dot(normed.reshape(CH_DEV * SEGMENTS, NSAMP), basis, preferred_element_type=jnp.float32)
        spec = spec.reshape(CH_DEV, SEGMENTS, 2 * BINS)
        sq = spec[..., :BINS] ** 2 + spec[..., BINS:] ** 2
        power = lax.optimization_barrier(jnp.sum(sq.reshape(CH_DEV, SEGMENTS, BINS // 16, 16), axis=(1, 3))) / (16.0 * SEGMENTS)
        scale = jnp.repeat(lax.rsqrt(power + 1e-06), 16, axis=1)
        scale = jnp.concatenate([scale, scale], axis=1)
        white = spec * scale[:, None, :] * flags.astype(jnp.float32)[:, None, None] * use_f[None, :, None]
        return white.astype(jnp.bfloat16)
    white = lax.map(whiten, (raw.reshape(blocks, CH_DEV, SEGMENTS, NSAMP), alive.reshape(blocks, CH_DEV)))
    white = white.reshape(CHANNELS, SEGMENTS, 2 * BINS)
    padded = jnp.pad(white, ((0, OFFS), (0, 0), (0, 0)))

    def cross(index):
        start = (index * CH_DEV).astype(jnp.int32)
        own = lax.dynamic_slice_in_dim(padded, start, CH_DEV, 0).astype(jnp.float32)
        ext = lax.dynamic_slice_in_dim(padded, start, CH_DEV + OFFS, 0).astype(jnp.float32)
        re_own, im_own = (own[..., :BINS], own[..., BINS:])
        re_ext, im_ext = (ext[..., :BINS], ext[..., BINS:])
        real = jnp.einsum('isf,jsf->ijf', re_own, re_ext) + jnp.einsum('isf,jsf->ijf', im_own, im_ext)
        imag = jnp.einsum('isf,jsf->ijf', im_own, re_ext) - jnp.einsum('isf,jsf->ijf', re_own, im_ext)
        both = jnp.concatenate([band_rows(real, CH_DEV, OFFS), band_rows(imag, CH_DEV, OFFS)], axis=-1)
        return (both * (1.0 / SEGMENTS)).astype(jnp.bfloat16)
    stack = lax.map(cross, jnp.arange(blocks, dtype=jnp.int32))
    return stack.reshape(CHANNELS, OFFS, 2 * BINS)
```

```python
import functools
import math

import jax
import jax.numpy as jnp
import numpy as np
from jax import lax
from jax.experimental import pallas as pl
from jax.experimental.pallas import tpu as pltpu
from jax.sharding import Mesh
from jax.sharding import PartitionSpec as P

BINS = 128
OFFS = 128
GROUP = 16
QUADS = 4
BATCHES = 2
F32 = jnp.float32
BF16 = jnp.bfloat16
VMEM = pl.BlockSpec(memory_space=pltpu.VMEM)
SMEM = pl.BlockSpec(memory_space=pltpu.SMEM)


def basis_columns(nsamp):
    times = np.arange(nsamp, dtype=np.int32)[:, None]
    freqs = np.arange(1, BINS + 1, dtype=np.int32)[None, :]
    phase = (times * freqs % nsamp).astype(np.float32) * np.float32(2.0 * math.pi / nsamp)
    scale = np.float32(1.0 / math.sqrt(nsamp))
    both = np.stack([np.cos(phase) * scale, -np.sin(phase) * scale], axis=-1)
    return jnp.asarray(both.reshape(nsamp, 2 * BINS), BF16)


def dot_nt(left, right):
    return lax.dot_general(left, right, (((1,), (1,)), ((), ())), preferred_element_type=F32)


def pack_kernel(use_ref, spec_ref, out_ref, scratch):
    segs, _, width = spec_ref.shape
    eye = (
        lax.broadcasted_iota(jnp.int32, (width, width), 0)
        == lax.broadcasted_iota(jnp.int32, (width, width), 1)
    ).astype(F32).astype(BF16)
    for seg in range(segs):
        scratch[pl.ds(seg, width, stride=segs), :] = dot_nt(eye, spec_ref[seg])
    rows = width * segs // QUADS
    seg_of_row = lax.broadcasted_iota(jnp.int32, (16, 128), 0) % segs
    flags = jnp.zeros((16, 128), F32)
    for seg in range(segs):
        flags = jnp.where(seg_of_row == seg, use_ref[seg].astype(F32), flags)
    for quad in range(QUADS):
        out_ref[quad, :16, :] = flags.astype(BF16)
        out_ref[quad, 16:, :] = scratch[quad * rows : (quad + 1) * rows, :].astype(BF16)


def stack_kernel(total_segs, par_ref, near_ref, far_ref, halo_ref, nflag_ref, fflag_ref, out_ref, scratch):
    half, swap, quad = par_ref[0], par_ref[1], par_ref[2]
    srcs, depth, width = near_ref.shape
    own_rows = 64

    def power(*parts):
        total = jnp.zeros((1, width), F32)
        for part in parts:
            value = part.astype(F32)
            total += jnp.sum(value * value, axis=(0, 1))[None, :]
        return lax.rsqrt(total * (1.0 / (GROUP * total_segs)) + 1e-06)

    own_scale = power(near_ref[...], far_ref[...])
    halo_scale = power(halo_ref[0], halo_ref[1])
    col_scale = jnp.concatenate([own_scale, halo_scale], axis=1) * (1.0 / total_segs)
    pick = lax.broadcasted_iota(jnp.int32, (own_rows, width), 1) == (
        64 * half + 63 - lax.broadcasted_iota(jnp.int32, (own_rows, width), 0)
    )
    row_scale = jnp.sum(jnp.where(pick, own_scale, 0.0), axis=1, keepdims=True)
    scale = row_scale * col_scale
    pick = pick.astype(F32).astype(BF16)

    row = lax.broadcasted_iota(jnp.int32, (128, 128), 0)
    col = lax.broadcasted_iota(jnp.int32, (128, 128), 1)
    flags = jnp.concatenate(
        [nflag_ref[src] for src in range(srcs)] + [fflag_ref[src] for src in range(srcs)], axis=0
    ).astype(F32)
    place = []
    for bin_ in range(2):
        keep = (col // 8) % 2 == bin_
        sign = jnp.where((col // 4) % 2 == 0, 1.0, -1.0)
        place.append(jnp.where(keep & (row == col), flags, 0.0))
        place.append(jnp.where(keep & (row == (col ^ 4)), flags * sign, 0.0))
    place = jnp.concatenate(place, axis=1).astype(BF16)

    def fill(which):
        for pair in range(GROUP // 2):
            rows = slice(16 * pair, 16 * pair + 16)
            own = jnp.concatenate(
                [near_ref[src, rows, :] for src in range(srcs)] + [far_ref[src, rows, :] for src in range(srcs)], axis=0
            )
            behind = jnp.concatenate(
                [halo_ref[swap, src, rows, :] for src in range(srcs)]
                + [halo_ref[1 - swap, src, rows, :] for src in range(srcs)],
                axis=0,
            )
            turned = dot_nt(pick, own).astype(BF16)
            left = jnp.dot(turned, place, preferred_element_type=F32).astype(BF16)
            left = jnp.concatenate([left[:, 128 * k : 128 * k + 128] for k in range(4)], axis=0)
            right = jnp.concatenate([own, behind], axis=1)
            both = jnp.dot(left, right, preferred_element_type=F32)
            for bin_ in range(2):
                for part in range(2):
                    k = 2 * bin_ + part
                    block = both[64 * k : 64 * k + 64] * scale
                    block = pltpu.roll(block, 193 - 64 * which, 1, stride=1, stride_axis=0)
                    scratch[pl.ds(part * 16 + 2 * pair + bin_, own_rows, stride=32), :] = block[:, :OFFS]

    for which in range(2):
        pl.when(half == which)(functools.partial(fill, which))
    for slot in range(QUADS):
        start = pl.multiple_of((3 - (quad ^ slot)) * 512, 512)
        out_ref[slot] = scratch[pl.ds(start, 512), :].astype(BF16)


def turn_kernel(par_ref, *refs):
    parts, out_ref, scratch = refs[:-2], refs[-2], refs[-1]
    quad = par_ref[2]
    count = out_ref.shape[0]
    eye = (
        lax.broadcasted_iota(jnp.int32, (128, 128), 0) == lax.broadcasted_iota(jnp.int32, (128, 128), 1)
    ).astype(F32).astype(BF16)
    for index, ref in enumerate(parts):
        batch, slot = index // QUADS, index % QUADS
        group = (quad ^ slot) * BATCHES + batch
        for row in range(count):
            for part in range(2):
                start = pl.multiple_of(part * 128 + GROUP * group, GROUP)
                scratch[count - 1 - row, pl.ds(start, GROUP), :] = ref[(2 * row + part) * 16 : (2 * row + part) * 16 + 16, :]
    for row in range(count):
        out_ref[row] = dot_nt(eye, scratch[row]).astype(BF16)


def shards(raw, alive, use):
    channels, seg_local, nsamp = raw.shape
    chans = lax.axis_size("chan")
    total_segs = seg_local * lax.axis_size("h") * lax.axis_size("q")
    axes = ("chan", "h", "q")
    me = lax.axis_index("chan")
    par = jnp.stack([lax.axis_index("h"), me % 2, lax.axis_index("q")]).astype(jnp.int32)

    meansq = jnp.mean(jnp.square(raw.astype(F32)), axis=-1, keepdims=True)
    scale = lax.rsqrt(meansq + 1e-06)
    spec = jnp.einsum("csn,nv->csv", raw, basis_columns(nsamp), preferred_element_type=F32)
    spec = jnp.where(scale > 0, spec * scale, 0.0) * alive.astype(F32)[:, None, None]
    spec = jnp.transpose(spec.astype(BF16), (1, 0, 2))
    rows = 2 * BINS * seg_local // QUADS
    message = pl.pallas_call(
        pack_kernel,
        out_shape=jax.ShapeDtypeStruct((QUADS, 16 + rows, channels), BF16),
        in_specs=[SMEM, VMEM],
        out_specs=VMEM,
        scratch_shapes=[pltpu.VMEM((rows * QUADS, channels), F32)],
        name="pack",
    )(use, spec)

    near = lax.all_to_all(message, "q", 0, 0, tiled=True)

    def index(chan, half, quad):
        return (chan * 2 + half) * QUADS + quad

    places = [(c, h, q) for c in range(chans) for h in range(2) for q in range(QUADS)]
    across = [(index(c, h, q), index(c, 1 - h, q)) for c, h, q in places]
    behind = [(index(c, h, q), index(c - 1, h if c % 2 else 1 - h, q)) for c, h, q in places if c > 0]
    batch_rows = rows // BATCHES
    near_parts = [near[:, : 16 + batch_rows], near[:, 16 + batch_rows :]]
    far_parts = [lax.ppermute(part, axes, across) for part in near_parts]
    near_flags, far_flags = near_parts[0][:, :16], far_parts[0][:, :16]
    near_parts[0], far_parts[0] = near_parts[0][:, 16:], far_parts[0][:, 16:]

    pieces = []
    for batch in range(BATCHES):
        own = jnp.stack([near_parts[batch], far_parts[batch]])
        halo = lax.ppermute(own, axes, behind)
        stacked = pl.pallas_call(
            functools.partial(stack_kernel, total_segs),
            out_shape=jax.ShapeDtypeStruct((QUADS, 512, OFFS), BF16),
            in_specs=[SMEM] + [VMEM] * 5,
            out_specs=VMEM,
            scratch_shapes=[pltpu.VMEM((512 * QUADS, OFFS), F32)],
            cost_estimate=pl.CostEstimate(flops=2 * 8 * 256 * 256 * 256, bytes_accessed=2**20, transcendentals=0),
            name="stack",
        )(par, near_parts[batch], far_parts[batch], halo, near_flags, far_flags)
        pieces.append(stacked[0])
        for slot in range(1, QUADS):
            pairs = [(index(c, h, q), index(c, h, q ^ slot)) for c, h, q in places]
            pieces.append(lax.ppermute(stacked[slot], axes, pairs))

    sub = channels // (2 * QUADS)
    steps = 4
    return pl.pallas_call(
        turn_kernel,
        out_shape=jax.ShapeDtypeStruct((sub, OFFS, 2 * BINS), BF16),
        grid=(steps,),
        in_specs=[SMEM] + [pl.BlockSpec((512 // steps, OFFS), lambda step: (steps - 1 - step, 0))] * len(pieces),
        out_specs=pl.BlockSpec((sub // steps, OFFS, 2 * BINS), lambda step: (step, 0, 0)),
        scratch_shapes=[pltpu.VMEM((sub // steps, 2 * BINS, OFFS), BF16)],
        name="turn",
    )(par, *pieces)


def solution(mesh):
    chans, groups = mesh.devices.shape
    fine = Mesh(mesh.devices.reshape(chans, 2, groups // 2), ("chan", "h", "q"))
    in_specs = (P("chan", ("h", "q"), None), P("chan"), P(("h", "q")))
    out_specs = P(("chan", "h", "q"), None, None)
    return jax.shard_map(shards, mesh=fine, in_specs=in_specs, out_specs=out_specs, check_vma=False)
```

```python
import functools
import math

import jax
import jax.numpy as jnp
import ml_dtypes
import numpy as np
from jax import lax
from jax.experimental import pallas as pl
from jax.experimental.pallas import tpu as pltpu
from jax.sharding import Mesh
from jax.sharding import PartitionSpec as P

BINS = 128
OFFS = 128
GROUP = 16
QUADS = 4
BATCHES = 2
FLAG_ROWS = 16
N_STEPS = 2
F32 = jnp.float32
BF16 = jnp.bfloat16
VMEM = pl.BlockSpec(memory_space=pltpu.VMEM)
SMEM = pl.BlockSpec(memory_space=pltpu.SMEM)
BIG = pltpu.CompilerParams(vmem_limit_bytes=60 * 2**20)


def basis_columns(nsamp):
    times = np.arange(nsamp, dtype=np.int32)[:, None]
    freqs = np.arange(1, BINS + 1, dtype=np.int32)[None, :]
    phase = (times * freqs % nsamp).astype(np.float32) * np.float32(2.0 * math.pi / nsamp)
    scale = np.float32(1.0 / math.sqrt(nsamp))
    both = np.stack([np.cos(phase) * scale, -np.sin(phase) * scale], axis=-1)
    return both.reshape(nsamp, 2 * BINS).astype(ml_dtypes.bfloat16)


def dot_nt(left, right):
    return lax.dot_general(left, right, (((1,), (1,)), ((), ())), preferred_element_type=F32)


def unit(size):
    rows = lax.broadcasted_iota(jnp.int32, (size, size), 0)
    return (rows == lax.broadcasted_iota(jnp.int32, (size, size), 1)).astype(F32).astype(BF16)


def spectrum_kernel(nsamp, use_ref, alive_ref, raw_ref, basis_ref, *refs):
    outs, (spec, square, turned) = refs[:-3], refs[-3:]
    channels, segs, part = raw_ref.shape
    step = pl.program_id(0)
    flat = raw_ref[...].reshape(channels * segs, part)
    signal = flat.astype(F32)
    signal = signal * signal
    squares = signal[:, :128]
    for col in range(128, part, 128):
        squares += signal[:, col : col + 128]
    product = jnp.dot(flat, basis_ref[...], preferred_element_type=F32)

    @pl.when(step == 0)
    def _():
        for col in range(2):
            spec[col] = product[:, 128 * col : 128 * col + 128]
        square[...] = squares

    @pl.when(step > 0)
    def _():
        for col in range(2):
            spec[col] += product[:, 128 * col : 128 * col + 128]
        square[...] += squares

    @pl.when(step == pl.num_programs(0) - 1)
    def _():
        meansq = jnp.sum(square[...], axis=1, keepdims=True) * (1.0 / nsamp)
        scale = lax.rsqrt(meansq + 1e-06)
        for col in range(2):
            spec[col] = jnp.where(scale > 0, spec[col] * scale, 0.0)
        width = 2 * 128
        alive = alive_ref[...].astype(F32)
        for seg in range(segs):
            rows = [spec[col, pl.ds(seg, channels, stride=segs), :].astype(BF16) for col in range(2)]
            rows = jnp.concatenate(rows, axis=1)
            turned[pl.ds(seg, width, stride=segs), :] = dot_nt(unit(width), rows) * alive
        seg_of_row = lax.broadcasted_iota(jnp.int32, (FLAG_ROWS, channels), 0) % segs
        flags = jnp.zeros((FLAG_ROWS, channels), F32)
        for seg in range(segs):
            flags = jnp.where(seg_of_row == seg, use_ref[seg].astype(F32), flags)
        flags = flags.astype(BF16)
        depth = width * segs // (QUADS * BATCHES)
        for quad in range(QUADS):
            for batch in range(BATCHES):
                start = (quad * BATCHES + batch) * depth
                value = turned[start : start + depth, :].astype(BF16)
                for half in range(2):
                    dest = half * QUADS + quad
                    if batch == 0:
                        outs[0][dest, :FLAG_ROWS, :] = flags
                        outs[0][dest, FLAG_ROWS:, :] = value
                    else:
                        outs[batch][dest] = value


def stack_kernel(total_segs, first, par_ref, own_ref, halo_ref, flag_ref, *refs):
    outs, scratch = refs[:QUADS], refs[QUADS]
    half, quad = par_ref[0], par_ref[1]
    srcs, _, width = own_ref.shape
    depth = GROUP * 8

    def inverse(ref):
        value = ref[:, first : first + depth, :].astype(F32)
        total = jnp.sum(value * value, axis=(0, 1))[None, :]
        return lax.rsqrt(total * (1.0 / (GROUP * total_segs)) + 1e-06)

    own_scale = inverse(own_ref)
    col_scale = jnp.concatenate([own_scale, inverse(halo_ref)], axis=1) * (1.0 / total_segs)
    pick = lax.broadcasted_iota(jnp.int32, (64, width), 1) == (
        64 * half + 63 - lax.broadcasted_iota(jnp.int32, (64, width), 0)
    )
    row_scale = jnp.sum(jnp.where(pick, own_scale, 0.0), axis=1, keepdims=True)
    scale = row_scale * col_scale
    pick = pick.astype(F32).astype(BF16)

    row = lax.broadcasted_iota(jnp.int32, (depth, depth), 0)
    col = lax.broadcasted_iota(jnp.int32, (depth, depth), 1)
    flags = flag_ref[:, :FLAG_ROWS, :].reshape(depth, width).astype(F32)
    place = []
    for bin_ in range(2):
        keep = (col // 8) % 2 == bin_
        sign = jnp.where((col // 4) % 2 == 0, 1.0, -1.0)
        place.append(jnp.where(keep & (row == col), flags, 0.0))
        place.append(jnp.where(keep & (row == (col ^ 4)), flags * sign, 0.0))
    place = jnp.concatenate(place, axis=1).astype(BF16)

    owns = []
    for pair in range(GROUP // 2):
        rows = slice(first + 16 * pair, first + 16 * pair + 16)
        owns.append(own_ref[:, rows, :].reshape(depth, width))
    turned = dot_nt(pick, jnp.concatenate(owns, axis=0)).astype(BF16)
    turned = jnp.concatenate([turned[:, depth * k : depth * k + depth] for k in range(GROUP // 2)], axis=0)
    lefts = jnp.dot(turned, place, preferred_element_type=F32).astype(BF16)

    def fill(which):
        for pair in range(GROUP // 2):
            rows = slice(first + 16 * pair, first + 16 * pair + 16)
            behind = halo_ref[:, rows, :].reshape(depth, width)
            left = lefts[64 * pair : 64 * pair + 64]
            left = jnp.concatenate([left[:, 128 * k : 128 * k + 128] for k in range(4)], axis=0)
            right = jnp.concatenate([owns[pair], behind], axis=1)
            both = jnp.dot(left, right, preferred_element_type=F32)
            for bin_ in range(2):
                for part in range(2):
                    k = 2 * bin_ + part
                    block = both[64 * k : 64 * k + 64] * scale
                    block = pltpu.roll(block, 193 - 64 * which, 1, stride=1, stride_axis=0)
                    scratch[pl.ds(part * 16 + 2 * pair + bin_, 64, stride=32), :] = block[:, :OFFS]

    for which in range(2):
        pl.when(half == which)(functools.partial(fill, which))
    for slot in range(QUADS):
        start = pl.multiple_of((3 - (quad ^ slot)) * 512, 512)
        outs[slot][...] = scratch[pl.ds(start, 512), :].astype(BF16)


def turn_kernel(par_ref, *refs):
    parts, out_ref, scratch = refs[:-2], refs[-2], refs[-1]
    quad = par_ref[1]
    count = out_ref.shape[0]
    for index, ref in enumerate(parts):
        batch, slot = index // QUADS, index % QUADS
        group = (quad ^ slot) * BATCHES + batch
        for row in range(count):
            for part in range(2):
                start = pl.multiple_of(part * 128 + GROUP * group, GROUP)
                begin = (2 * row + part) * GROUP
                scratch[count - 1 - row, pl.ds(start, GROUP), :] = ref[begin : begin + GROUP, :]
    eye = unit(OFFS)
    for row in range(count):
        out_ref[row] = dot_nt(eye, scratch[row]).astype(BF16)


def spectra(raw, alive, use):
    channels, segs, nsamp = raw.shape
    depth = 2 * BINS * segs // (QUADS * BATCHES)
    part = nsamp // N_STEPS
    return pl.pallas_call(
        functools.partial(spectrum_kernel, nsamp),
        out_shape=[
            jax.ShapeDtypeStruct((2 * QUADS, depth + (FLAG_ROWS if batch == 0 else 0), channels), BF16)
            for batch in range(BATCHES)
        ],
        grid=(N_STEPS,),
        in_specs=[
            SMEM,
            VMEM,
            pl.BlockSpec((channels, segs, part), lambda step: (0, 0, step)),
            pl.BlockSpec((part, 2 * BINS), lambda step: (step, 0)),
        ],
        out_specs=[VMEM] * BATCHES,
        scratch_shapes=[
            pltpu.VMEM((2, channels * segs, BINS), F32),
            pltpu.VMEM((channels * segs, 128), F32),
            pltpu.VMEM((2 * BINS * segs, channels), F32),
        ],
        compiler_params=BIG,
        name="spectra",
    )(use, alive[None, :], raw, basis_columns(nsamp))


def stack_pairs(par, own, halo, flags, total_segs, first):
    return pl.pallas_call(
        functools.partial(stack_kernel, total_segs, first),
        out_shape=[jax.ShapeDtypeStruct((512, OFFS), BF16)] * QUADS,
        in_specs=[SMEM] + [VMEM] * 3,
        out_specs=[VMEM] * QUADS,
        scratch_shapes=[pltpu.VMEM((512 * QUADS, OFFS), F32)],
        cost_estimate=pl.CostEstimate(flops=2 * 8 * 256 * 256 * 256, bytes_accessed=2**20, transcendentals=0),
        name="stack",
    )(par, own, halo, flags)


def turn_pieces(par, pieces, sub):
    steps = 2
    return pl.pallas_call(
        turn_kernel,
        out_shape=jax.ShapeDtypeStruct((sub, OFFS, 2 * BINS), BF16),
        grid=(steps,),
        in_specs=[SMEM] + [pl.BlockSpec((512 // steps, OFFS), lambda step: (steps - 1 - step, 0))] * len(pieces),
        out_specs=pl.BlockSpec((sub // steps, OFFS, 2 * BINS), lambda step: (step, 0, 0)),
        scratch_shapes=[pltpu.VMEM((sub // steps, 2 * BINS, OFFS), BF16)],
        name="turn",
    )(par, *pieces)


def shards(raw, alive, use):
    channels, seg_local, _ = raw.shape
    chans = lax.axis_size("chan")
    total_segs = seg_local * lax.axis_size("h") * lax.axis_size("q")
    axes = ("chan", "h", "q")
    par = jnp.stack([lax.axis_index("h"), lax.axis_index("q")]).astype(jnp.int32)

    def index(chan, half, quad):
        return (chan * 2 + half) * QUADS + quad

    places = [(c, h, q) for c in range(chans) for h in range(2) for q in range(QUADS)]
    behind = [(index(c, h, q), index(c - 1, h if c % 2 else 1 - h, q)) for c, h, q in places if c > 0]

    owns = [lax.all_to_all(message, ("h", "q"), 0, 0, tiled=True) for message in spectra(raw, alive, use)]
    halos = [lax.ppermute(own, axes, behind) for own in owns]
    pieces = []
    for batch, (own, halo) in enumerate(zip(owns, halos)):
        first = FLAG_ROWS if batch == 0 else 0
        stacked = stack_pairs(par, own, halo, owns[0], total_segs, first)
        part = [stacked[0]] + [None] * (QUADS - 1)
        for slot in (2, 3, 1):
            pairs = [(index(c, h, q), index(c, h, q ^ slot)) for c, h, q in places]
            part[slot] = lax.ppermute(stacked[slot], axes, pairs)
        pieces += part
    return turn_pieces(par, pieces, channels // (2 * QUADS))


def solution(mesh):
    chans, groups = mesh.devices.shape
    fine = Mesh(mesh.devices.reshape(chans, 2, groups // 2), ("chan", "h", "q"))
    in_specs = (P("chan", ("h", "q"), None), P("chan"), P(("h", "q")))
    out_specs = P(("chan", "h", "q"), None, None)
    return jax.shard_map(shards, mesh=fine, in_specs=in_specs, out_specs=out_specs, check_vma=False)
```

```python
import functools
import math

import jax
import jax.numpy as jnp
import ml_dtypes
import numpy as np
from jax import lax
from jax.experimental import pallas as pl
from jax.experimental.pallas import tpu as pltpu
from jax.sharding import Mesh
from jax.sharding import PartitionSpec as P

BINS = 128
OFFS = 128
GROUP = 16
QUADS = 4
BATCHES = 2
FLAG_ROWS = 16
N_STEPS = 2
F32 = jnp.float32
BF16 = jnp.bfloat16
VMEM = pl.BlockSpec(memory_space=pltpu.VMEM)
SMEM = pl.BlockSpec(memory_space=pltpu.SMEM)
SMALL = pltpu.CompilerParams(vmem_limit_bytes=16 * 2**20)
BIG = pltpu.CompilerParams(vmem_limit_bytes=60 * 2**20)


def basis_columns(nsamp):
    times = np.arange(nsamp, dtype=np.int32)[:, None]
    freqs = np.arange(1, BINS + 1, dtype=np.int32)[None, :]
    phase = (times * freqs % nsamp).astype(np.float32) * np.float32(2.0 * math.pi / nsamp)
    scale = np.float32(1.0 / math.sqrt(nsamp))
    both = np.stack([np.cos(phase) * scale, -np.sin(phase) * scale], axis=-1)
    return both.reshape(nsamp, 2 * BINS).astype(ml_dtypes.bfloat16)


def dot_nt(left, right):
    return lax.dot_general(left, right, (((1,), (1,)), ((), ())), preferred_element_type=F32)


def unit(size):
    rows = lax.broadcasted_iota(jnp.int32, (size, size), 0)
    return (rows == lax.broadcasted_iota(jnp.int32, (size, size), 1)).astype(F32).astype(BF16)


def spectrum_kernel(nsamp, use_ref, alive_ref, raw_ref, basis_ref, *refs):
    outs, (spec, square, turned) = refs[:-3], refs[-3:]
    channels, segs, part = raw_ref.shape
    step = pl.program_id(0)
    flat = raw_ref[...].reshape(channels * segs, part)
    signal = flat.astype(F32)
    signal = signal * signal
    squares = signal[:, :128]
    for col in range(128, part, 128):
        squares += signal[:, col : col + 128]
    product = jnp.dot(flat, basis_ref[...], preferred_element_type=F32)

    @pl.when(step == 0)
    def _():
        for col in range(2):
            spec[col] = product[:, 128 * col : 128 * col + 128]
        square[...] = squares

    @pl.when(step > 0)
    def _():
        for col in range(2):
            spec[col] += product[:, 128 * col : 128 * col + 128]
        square[...] += squares

    @pl.when(step == pl.num_programs(0) - 1)
    def _():
        meansq = jnp.sum(square[...], axis=1, keepdims=True) * (1.0 / nsamp)
        scale = lax.rsqrt(meansq + 1e-06)
        for col in range(2):
            spec[col] = jnp.where(scale > 0, spec[col] * scale, 0.0)
        width = 2 * 128
        alive = alive_ref[...].astype(F32)
        for seg in range(segs):
            rows = [spec[col, pl.ds(seg, channels, stride=segs), :].astype(BF16) for col in range(2)]
            rows = jnp.concatenate(rows, axis=1)
            turned[pl.ds(seg, width, stride=segs), :] = dot_nt(unit(width), rows) * alive
        seg_of_row = lax.broadcasted_iota(jnp.int32, (FLAG_ROWS, channels), 0) % segs
        flags = jnp.zeros((FLAG_ROWS, channels), F32)
        for seg in range(segs):
            flags = jnp.where(seg_of_row == seg, use_ref[seg].astype(F32), flags)
        flags = flags.astype(BF16)
        depth = width * segs // (QUADS * BATCHES)
        for quad in range(QUADS):
            for batch in range(BATCHES):
                start = (quad * BATCHES + batch) * depth
                value = turned[start : start + depth, :].astype(BF16)
                for half in range(2):
                    dest = half * QUADS + quad
                    if batch == 0:
                        outs[0][dest, :FLAG_ROWS, :] = flags
                        outs[0][dest, FLAG_ROWS:, :] = value
                    else:
                        outs[batch][dest] = value


def stack_kernel(total_segs, first, own_ref, halo_ref, flag_ref, *refs):
    outs, scratch = refs[:-1], refs[-1]
    half, quad = lax.axis_index("h"), lax.axis_index("q")
    srcs, _, width = own_ref.shape
    depth = GROUP * 8

    def inverse(ref):
        value = ref[:, first : first + depth, :].astype(F32)
        total = jnp.sum(value * value, axis=(0, 1))[None, :]
        return lax.rsqrt(total * (1.0 / (GROUP * total_segs)) + 1e-06)

    own_scale = inverse(own_ref)
    col_scale = jnp.concatenate([own_scale, inverse(halo_ref)], axis=1) * (1.0 / total_segs)
    pick = lax.broadcasted_iota(jnp.int32, (64, width), 1) == (
        64 * half + 63 - lax.broadcasted_iota(jnp.int32, (64, width), 0)
    )
    row_scale = jnp.sum(jnp.where(pick, own_scale, 0.0), axis=1, keepdims=True)
    scale = row_scale * col_scale
    pick = pick.astype(F32).astype(BF16)

    row = lax.broadcasted_iota(jnp.int32, (depth, depth), 0)
    col = lax.broadcasted_iota(jnp.int32, (depth, depth), 1)
    flags = flag_ref[:, :FLAG_ROWS, :].reshape(depth, width).astype(F32)
    place = []
    for bin_ in range(2):
        keep = (col // 8) % 2 == bin_
        sign = jnp.where((col // 4) % 2 == 0, 1.0, -1.0)
        place.append(jnp.where(keep & (row == col), flags, 0.0))
        place.append(jnp.where(keep & (row == (col ^ 4)), flags * sign, 0.0))
    place = jnp.concatenate(place, axis=1).astype(BF16)

    owns = []
    for pair in range(GROUP // 2):
        rows = slice(first + 16 * pair, first + 16 * pair + 16)
        owns.append(own_ref[:, rows, :].reshape(depth, width))
    turned = dot_nt(pick, jnp.concatenate(owns, axis=0)).astype(BF16)
    turned = jnp.concatenate([turned[:, depth * k : depth * k + depth] for k in range(GROUP // 2)], axis=0)
    lefts = jnp.dot(turned, place, preferred_element_type=F32).astype(BF16)

    def fill(which):
        for pair in range(GROUP // 2):
            rows = slice(first + 16 * pair, first + 16 * pair + 16)
            behind = halo_ref[:, rows, :].reshape(depth, width)
            left = lefts[64 * pair : 64 * pair + 64]
            left = jnp.concatenate([left[:, 128 * k : 128 * k + 128] for k in range(4)], axis=0)
            right = jnp.concatenate([owns[pair], behind], axis=1)
            both = jnp.dot(left, right, preferred_element_type=F32)
            for bin_ in range(2):
                for part in range(2):
                    k = 2 * bin_ + part
                    block = both[64 * k : 64 * k + 64] * scale
                    block = pltpu.roll(block, 193 - 64 * which, 1, stride=1, stride_axis=0)
                    scratch[pl.ds(part * 16 + 2 * pair + bin_, 64, stride=32), :] = block[:, :OFFS]

    for which in range(2):
        pl.when(half == which)(functools.partial(fill, which))
    for slot in range(QUADS):
        if len(outs) == 1:
            outs[0][slot] = scratch[(3 - slot) * 512 : (4 - slot) * 512, :].astype(BF16)
        else:
            start = pl.multiple_of((3 - (quad ^ slot)) * 512, 512)
            outs[slot][...] = scratch[pl.ds(start, 512), :].astype(BF16)


def turn_kernel(*refs):
    parts, out_ref, scratch = refs[:-2], refs[-2], refs[-1]
    quad = lax.axis_index("q")
    count = out_ref.shape[0]
    sources = [(quad ^ slot, 0, ref) for slot, ref in enumerate(parts[:QUADS])]
    sources += [(source, 1, parts[QUADS].at[source]) for source in range(QUADS)]
    for source, batch, ref in sources:
        group = source * BATCHES + batch
        for row in range(count):
            for part in range(2):
                start = pl.multiple_of(part * 128 + GROUP * group, GROUP)
                begin = (2 * row + part) * GROUP
                scratch[count - 1 - row, pl.ds(start, GROUP), :] = ref[begin : begin + GROUP, :]
    eye = unit(OFFS)
    for row in range(count):
        out_ref[row] = dot_nt(eye, scratch[row]).astype(BF16)


def spectra(raw, alive, use):
    channels, segs, nsamp = raw.shape
    depth = 2 * BINS * segs // (QUADS * BATCHES)
    part = nsamp // N_STEPS
    return pl.pallas_call(
        functools.partial(spectrum_kernel, nsamp),
        out_shape=[
            jax.ShapeDtypeStruct((2 * QUADS, depth + (FLAG_ROWS if batch == 0 else 0), channels), BF16)
            for batch in range(BATCHES)
        ],
        grid=(N_STEPS,),
        in_specs=[
            SMEM,
            VMEM,
            pl.BlockSpec((channels, segs, part), lambda step: (0, 0, step)),
            pl.BlockSpec((part, 2 * BINS), lambda step: (step, 0)),
        ],
        out_specs=[VMEM] * BATCHES,
        scratch_shapes=[
            pltpu.VMEM((2, channels * segs, BINS), F32),
            pltpu.VMEM((channels * segs, 128), F32),
            pltpu.VMEM((2 * BINS * segs, channels), F32),
        ],
        compiler_params=BIG,
        name="spectra",
    )(use, alive[None, :], raw, basis_columns(nsamp))


def stack_pairs(own, halo, flags, total_segs, first):
    if first == 0:
        shapes = [jax.ShapeDtypeStruct((QUADS, 512, OFFS), BF16)]
    else:
        shapes = [jax.ShapeDtypeStruct((512, OFFS), BF16)] * QUADS
    return pl.pallas_call(
        functools.partial(stack_kernel, total_segs, first),
        out_shape=shapes,
        in_specs=[VMEM] * 3,
        out_specs=[VMEM] * len(shapes),
        scratch_shapes=[pltpu.VMEM((512 * QUADS, OFFS), F32)],
        cost_estimate=pl.CostEstimate(flops=2 * 8 * 256 * 256 * 256 * 100, bytes_accessed=100 * 2**20, transcendentals=0),
        compiler_params=SMALL,
        name="stack",
    )(own, halo, flags)


def turn_pieces(pieces, sub):
    steps = 2
    return pl.pallas_call(
        turn_kernel,
        out_shape=jax.ShapeDtypeStruct((sub, OFFS, 2 * BINS), BF16),
        grid=(steps,),
        in_specs=[pl.BlockSpec((512 // steps, OFFS), lambda step: (steps - 1 - step, 0))] * QUADS
        + [pl.BlockSpec((QUADS, 512 // steps, OFFS), lambda step: (0, steps - 1 - step, 0))],
        out_specs=pl.BlockSpec((sub // steps, OFFS, 2 * BINS), lambda step: (step, 0, 0)),
        scratch_shapes=[pltpu.VMEM((sub // steps, 2 * BINS, OFFS), BF16)],
        compiler_params=SMALL,
        name="turn",
    )(*pieces)


def shards(raw, alive, use):
    channels, seg_local, _ = raw.shape
    chans = lax.axis_size("chan")
    total_segs = seg_local * lax.axis_size("h") * lax.axis_size("q")
    axes = ("chan", "h", "q")

    def index(chan, half, quad):
        return (chan * 2 + half) * QUADS + quad

    places = [(c, h, q) for c in range(chans) for h in range(2) for q in range(QUADS)]
    behind = [(index(c, h, q), index(c - 1, h if c % 2 else 1 - h, q)) for c, h, q in places if c > 0]

    owns = [lax.all_to_all(message, ("h", "q"), 0, 0, tiled=True) for message in spectra(raw, alive, use)]
    halos = [lax.ppermute(own, axes, behind) for own in owns]
    pieces = []
    for batch, (own, halo) in enumerate(zip(owns, halos)):
        first = FLAG_ROWS if batch == 0 else 0
        stacked = stack_pairs(own, halo, owns[0], total_segs, first)
        if batch == 1:
            pieces.append(lax.all_to_all(stacked[0], "q", 0, 0, tiled=True))
            continue
        part = [stacked[0]] + [None] * (QUADS - 1)
        for slot in (2, 3, 1):
            pairs = [(index(c, h, q), index(c, h, q ^ slot)) for c, h, q in places]
            part[slot] = lax.ppermute(stacked[slot], axes, pairs)
        pieces += part
    return turn_pieces(pieces, channels // (2 * QUADS))


def solution(mesh):
    chans, groups = mesh.devices.shape
    fine = Mesh(mesh.devices.reshape(chans, 2, groups // 2), ("chan", "h", "q"))
    in_specs = (P("chan", ("h", "q"), None), P("chan"), P(("h", "q")))
    out_specs = P(("chan", "h", "q"), None, None)
    return jax.shard_map(shards, mesh=fine, in_specs=in_specs, out_specs=out_specs, check_vma=False)
```

```python
import functools
import math

import jax
import jax.numpy as jnp
import ml_dtypes
import numpy as np
from jax import lax
from jax.experimental import pallas as pl
from jax.experimental.pallas import tpu as pltpu
from jax.sharding import Mesh
from jax.sharding import PartitionSpec as P

BINS = 128
OFFS = 128
GROUP = 16
QUADS = 4
BATCHES = 2
FLAG_ROWS = 16
N_STEPS = 2
F32 = jnp.float32
BF16 = jnp.bfloat16
VMEM = pl.BlockSpec(memory_space=pltpu.VMEM)
SMEM = pl.BlockSpec(memory_space=pltpu.SMEM)
SMALL = pltpu.CompilerParams(vmem_limit_bytes=16 * 2**20)
BIG = pltpu.CompilerParams(vmem_limit_bytes=60 * 2**20)


def basis_columns(nsamp):
    times = np.arange(nsamp, dtype=np.int32)[:, None]
    freqs = np.arange(1, BINS + 1, dtype=np.int32)[None, :]
    phase = (times * freqs % nsamp).astype(np.float32) * np.float32(2.0 * math.pi / nsamp)
    scale = np.float32(1.0 / math.sqrt(nsamp))
    both = np.stack([np.cos(phase) * scale, -np.sin(phase) * scale], axis=-1)
    return both.reshape(nsamp, 2 * BINS).astype(ml_dtypes.bfloat16)


def dot_nt(left, right):
    return lax.dot_general(left, right, (((1,), (1,)), ((), ())), preferred_element_type=F32)


def unit(size):
    rows = lax.broadcasted_iota(jnp.int32, (size, size), 0)
    return (rows == lax.broadcasted_iota(jnp.int32, (size, size), 1)).astype(F32).astype(BF16)


def spectrum_kernel(nsamp, use_ref, alive_ref, raw_ref, basis_ref, *refs):
    outs, (spec, square, turned) = refs[:-3], refs[-3:]
    channels, segs, part = raw_ref.shape
    step = pl.program_id(0)
    flat = raw_ref[...].reshape(channels * segs, part)
    signal = flat.astype(F32)
    signal = signal * signal
    squares = signal[:, :128]
    for col in range(128, part, 128):
        squares += signal[:, col : col + 128]
    product = jnp.dot(flat, basis_ref[...], preferred_element_type=F32)

    @pl.when(step == 0)
    def _():
        for col in range(2):
            spec[col] = product[:, 128 * col : 128 * col + 128]
        square[...] = squares

    @pl.when(step > 0)
    def _():
        for col in range(2):
            spec[col] += product[:, 128 * col : 128 * col + 128]
        square[...] += squares

    @pl.when(step == pl.num_programs(0) - 1)
    def _():
        meansq = jnp.sum(square[...], axis=1, keepdims=True) * (1.0 / nsamp)
        scale = lax.rsqrt(meansq + 1e-06)
        for col in range(2):
            spec[col] = jnp.where(scale > 0, spec[col] * scale, 0.0)
        width = 2 * 128
        alive = alive_ref[...].astype(F32)
        for seg in range(segs):
            rows = [spec[col, pl.ds(seg, channels, stride=segs), :].astype(BF16) for col in range(2)]
            rows = jnp.concatenate(rows, axis=1)
            turned[pl.ds(seg, width, stride=segs), :] = dot_nt(unit(width), rows) * alive
        seg_of_row = lax.broadcasted_iota(jnp.int32, (FLAG_ROWS, channels), 0) % segs
        flags = jnp.zeros((FLAG_ROWS, channels), F32)
        for seg in range(segs):
            flags = jnp.where(seg_of_row == seg, use_ref[seg].astype(F32), flags)
        flags = flags.astype(BF16)
        depth = width * segs // (QUADS * BATCHES)
        for quad in range(QUADS):
            for batch in range(BATCHES):
                start = (quad * BATCHES + batch) * depth
                value = turned[start : start + depth, :].astype(BF16)
                for half in range(2):
                    dest = half * QUADS + quad
                    if batch == 0:
                        outs[0][dest, :FLAG_ROWS, :] = flags
                        outs[0][dest, FLAG_ROWS:, :] = value
                    else:
                        outs[batch][dest] = value


def stack_kernel(total_segs, first, own_ref, halo_ref, flag_ref, *refs):
    outs, scratch = refs[:-1], refs[-1]
    half, quad = lax.axis_index("h"), lax.axis_index("q")
    srcs, _, width = own_ref.shape
    depth = GROUP * 8

    def inverse(value):
        value = value.astype(F32)
        total = jnp.sum(value * value, axis=(0, 1))[None, :]
        return lax.rsqrt(total * (1.0 / (GROUP * total_segs)) + 1e-06)

    own_scale = inverse(own_ref[:, first : first + depth, :])
    col_scale = jnp.concatenate([own_scale, inverse(halo_ref[...])], axis=1) * (1.0 / total_segs)
    pick = lax.broadcasted_iota(jnp.int32, (64, width), 1) == (
        64 * half + 63 - lax.broadcasted_iota(jnp.int32, (64, width), 0)
    )
    row_scale = jnp.sum(jnp.where(pick, own_scale, 0.0), axis=1, keepdims=True)
    scale = row_scale * col_scale
    pick = pick.astype(F32).astype(BF16)

    row = lax.broadcasted_iota(jnp.int32, (depth, depth), 0)
    col = lax.broadcasted_iota(jnp.int32, (depth, depth), 1)
    flags = flag_ref[:, :FLAG_ROWS, :].reshape(depth, width).astype(F32)
    place = []
    for bin_ in range(2):
        keep = (col // 8) % 2 == bin_
        sign = jnp.where((col // 4) % 2 == 0, 1.0, -1.0)
        place.append(jnp.where(keep & (row == col), flags, 0.0))
        place.append(jnp.where(keep & (row == (col ^ 4)), flags * sign, 0.0))
    place = jnp.concatenate(place, axis=1).astype(BF16)

    owns = []
    for pair in range(GROUP // 2):
        rows = slice(first + 16 * pair, first + 16 * pair + 16)
        owns.append(own_ref[:, rows, :].reshape(depth, width))
    turned = dot_nt(pick, jnp.concatenate(owns, axis=0)).astype(BF16)
    turned = jnp.concatenate([turned[:, depth * k : depth * k + depth] for k in range(GROUP // 2)], axis=0)
    lefts = jnp.dot(turned, place, preferred_element_type=F32).astype(BF16)

    def fill(which):
        for pair in range(GROUP // 2):
            rows = slice(first + 16 * pair, first + 16 * pair + 16)
            behind = halo_ref[:, 16 * pair : 16 * pair + 16, :].reshape(depth, width)
            left = lefts[64 * pair : 64 * pair + 64]
            left = jnp.concatenate([left[:, 128 * k : 128 * k + 128] for k in range(4)], axis=0)
            right = jnp.concatenate([owns[pair], behind], axis=1)
            both = jnp.dot(left, right, preferred_element_type=F32)
            for bin_ in range(2):
                for part in range(2):
                    k = 2 * bin_ + part
                    block = both[64 * k : 64 * k + 64] * scale
                    block = pltpu.roll(block, 193 - 64 * which, 1, stride=1, stride_axis=0)
                    scratch[pl.ds(part * 16 + 2 * pair + bin_, 64, stride=32), :] = block[:, :OFFS]

    for which in range(2):
        pl.when(half == which)(functools.partial(fill, which))
    for slot in range(QUADS):
        if len(outs) == 1:
            outs[0][slot] = scratch[(3 - slot) * 512 : (4 - slot) * 512, :].astype(BF16)
        else:
            start = pl.multiple_of((3 - (quad ^ slot)) * 512, 512)
            outs[slot][...] = scratch[pl.ds(start, 512), :].astype(BF16)


def turn_kernel(*refs):
    parts, out_ref, scratch = refs[:-2], refs[-2], refs[-1]
    quad = lax.axis_index("q")
    count = out_ref.shape[0]
    sources = [(quad ^ slot, 0, ref) for slot, ref in enumerate(parts[:QUADS])]
    sources += [(source, 1, parts[QUADS].at[source]) for source in range(QUADS)]
    for source, batch, ref in sources:
        group = source * BATCHES + batch
        for row in range(count):
            for part in range(2):
                start = pl.multiple_of(part * 128 + GROUP * group, GROUP)
                begin = (2 * row + part) * GROUP
                scratch[count - 1 - row, pl.ds(start, GROUP), :] = ref[begin : begin + GROUP, :]
    eye = unit(OFFS)
    for row in range(count):
        out_ref[row] = dot_nt(eye, scratch[row]).astype(BF16)


def spectra(raw, alive, use):
    channels, segs, nsamp = raw.shape
    depth = 2 * BINS * segs // (QUADS * BATCHES)
    part = nsamp // N_STEPS
    return pl.pallas_call(
        functools.partial(spectrum_kernel, nsamp),
        out_shape=[
            jax.ShapeDtypeStruct((2 * QUADS, depth + (FLAG_ROWS if batch == 0 else 0), channels), BF16)
            for batch in range(BATCHES)
        ],
        grid=(N_STEPS,),
        in_specs=[
            SMEM,
            VMEM,
            pl.BlockSpec((channels, segs, part), lambda step: (0, 0, step)),
            pl.BlockSpec((part, 2 * BINS), lambda step: (step, 0)),
        ],
        out_specs=[VMEM] * BATCHES,
        scratch_shapes=[
            pltpu.VMEM((2, channels * segs, BINS), F32),
            pltpu.VMEM((channels * segs, 128), F32),
            pltpu.VMEM((2 * BINS * segs, channels), F32),
        ],
        compiler_params=BIG,
        name="spectra",
    )(use, alive[None, :], raw, basis_columns(nsamp))


def stack_pairs(own, halo, flags, total_segs, first):
    if first == 0:
        shapes = [jax.ShapeDtypeStruct((QUADS, 512, OFFS), BF16)]
    else:
        shapes = [jax.ShapeDtypeStruct((512, OFFS), BF16)] * QUADS
    return pl.pallas_call(
        functools.partial(stack_kernel, total_segs, first),
        out_shape=shapes,
        in_specs=[VMEM] * 3,
        out_specs=[VMEM] * len(shapes),
        scratch_shapes=[pltpu.VMEM((512 * QUADS, OFFS), F32)],
        cost_estimate=pl.CostEstimate(flops=2 * 8 * 256 * 256 * 256 * 100, bytes_accessed=100 * 2**20, transcendentals=0),
        compiler_params=SMALL,
        name="stack",
    )(own, halo, flags)


def turn_pieces(pieces, sub):
    steps = 2
    return pl.pallas_call(
        turn_kernel,
        out_shape=jax.ShapeDtypeStruct((sub, OFFS, 2 * BINS), BF16),
        grid=(steps,),
        in_specs=[pl.BlockSpec((512 // steps, OFFS), lambda step: (steps - 1 - step, 0))] * QUADS
        + [pl.BlockSpec((QUADS, 512 // steps, OFFS), lambda step: (0, steps - 1 - step, 0))],
        out_specs=pl.BlockSpec((sub // steps, OFFS, 2 * BINS), lambda step: (step, 0, 0)),
        scratch_shapes=[pltpu.VMEM((sub // steps, 2 * BINS, OFFS), BF16)],
        compiler_params=SMALL,
        name="turn",
    )(*pieces)


def shards(raw, alive, use):
    channels, seg_local, _ = raw.shape
    chans = lax.axis_size("chan")
    total_segs = seg_local * lax.axis_size("h") * lax.axis_size("q")
    axes = ("chan", "h", "q")

    def index(chan, half, quad):
        return (chan * 2 + half) * QUADS + quad

    places = [(c, h, q) for c in range(chans) for h in range(2) for q in range(QUADS)]
    behind = [(index(c, h, q), index(c - 1, h if c % 2 else 1 - h, q)) for c, h, q in places if c > 0]

    owns = [lax.all_to_all(message, ("h", "q"), 0, 0, tiled=True) for message in spectra(raw, alive, use)]
    halos = [lax.ppermute(own[:, -GROUP * 8 :], axes, behind) for own in owns]
    pieces = []
    for batch, (own, halo) in enumerate(zip(owns, halos)):
        first = FLAG_ROWS if batch == 0 else 0
        stacked = stack_pairs(own, halo, owns[0], total_segs, first)
        if batch == 1:
            pieces.append(lax.all_to_all(stacked[0], "q", 0, 0, tiled=True))
            continue
        part = [stacked[0]] + [None] * (QUADS - 1)
        for slot in (2, 3, 1):
            pairs = [(index(c, h, q), index(c, h, q ^ slot)) for c, h, q in places]
            part[slot] = lax.ppermute(stacked[slot], axes, pairs)
        pieces += part
    return turn_pieces(pieces, channels // (2 * QUADS))


def solution(mesh):
    chans, groups = mesh.devices.shape
    fine = Mesh(mesh.devices.reshape(chans, 2, groups // 2), ("chan", "h", "q"))
    in_specs = (P("chan", ("h", "q"), None), P("chan"), P(("h", "q")))
    out_specs = P(("chan", "h", "q"), None, None)
    return jax.shard_map(shards, mesh=fine, in_specs=in_specs, out_specs=out_specs, check_vma=False)
```

```python
import functools
import math

import jax
import jax.numpy as jnp
import ml_dtypes
import numpy as np
from jax import lax
from jax.experimental import pallas as pl
from jax.experimental.pallas import tpu as pltpu
from jax.sharding import Mesh
from jax.sharding import PartitionSpec as P

BINS = 128
OFFS = 128
GROUP = 16
QUADS = 4
BATCHES = 2
FLAG_ROWS = 16
N_STEPS = 2
F32 = jnp.float32
BF16 = jnp.bfloat16
VMEM = pl.BlockSpec(memory_space=pltpu.VMEM)
SMEM = pl.BlockSpec(memory_space=pltpu.SMEM)
SMALL = pltpu.CompilerParams(vmem_limit_bytes=16 * 2**20)
BIG = pltpu.CompilerParams(vmem_limit_bytes=60 * 2**20)


def basis_columns(nsamp):
    times = np.arange(nsamp, dtype=np.int32)[:, None]
    freqs = np.arange(1, BINS + 1, dtype=np.int32)[None, :]
    phase = (times * freqs % nsamp).astype(np.float32) * np.float32(2.0 * math.pi / nsamp)
    scale = np.float32(1.0 / math.sqrt(nsamp))
    both = np.stack([np.cos(phase) * scale, -np.sin(phase) * scale], axis=-1)
    return both.reshape(nsamp, 2 * BINS).astype(ml_dtypes.bfloat16)


def dot_nt(left, right):
    return lax.dot_general(left, right, (((1,), (1,)), ((), ())), preferred_element_type=F32)


def unit(size):
    rows = lax.broadcasted_iota(jnp.int32, (size, size), 0)
    return (rows == lax.broadcasted_iota(jnp.int32, (size, size), 1)).astype(F32).astype(BF16)


def spectrum_kernel(nsamp, use_ref, alive_ref, raw_ref, basis_ref, *refs):
    outs, (spec, square, turned) = refs[:-3], refs[-3:]
    channels, segs, part = raw_ref.shape
    step = pl.program_id(0)
    flat = raw_ref[...].reshape(channels * segs, part)
    signal = flat.astype(F32)
    signal = signal * signal
    squares = signal[:, :128]
    for col in range(128, part, 128):
        squares += signal[:, col : col + 128]
    product = jnp.dot(flat, basis_ref[...], preferred_element_type=F32)

    @pl.when(step == 0)
    def _():
        for col in range(2):
            spec[col, : channels * segs] = product[:, 128 * col : 128 * col + 128]
        square[...] = squares

    @pl.when(step > 0)
    def _():
        for col in range(2):
            spec[col, : channels * segs] += product[:, 128 * col : 128 * col + 128]
        square[...] += squares

    @pl.when(step == pl.num_programs(0) - 1)
    def _():
        meansq = jnp.sum(square[...], axis=1, keepdims=True) * (1.0 / nsamp)
        scale = lax.rsqrt(meansq + 1e-06)
        for col in range(2):
            spec[col, : channels * segs] = jnp.where(scale > 0, spec[col, : channels * segs] * scale, 0.0)
        width = 2 * 128
        alive = alive_ref[...].astype(F32)
        for seg in range(segs):
            rows = [spec[col, pl.ds(seg, channels, stride=segs), :].astype(BF16) for col in range(2)]
            rows = jnp.concatenate(rows, axis=1)
            turned[pl.ds(seg, width, stride=segs), :] = dot_nt(unit(width), rows) * alive
        seg_of_row = lax.broadcasted_iota(jnp.int32, (FLAG_ROWS, channels), 0) % segs
        flags = jnp.zeros((FLAG_ROWS, channels), F32)
        for seg in range(segs):
            flags = jnp.where(seg_of_row == seg, use_ref[seg].astype(F32), flags)
        flags = flags.astype(BF16)
        depth = width * segs // (QUADS * BATCHES)
        for quad in range(QUADS):
            for batch in range(BATCHES):
                start = (quad * BATCHES + batch) * depth
                value = turned[start : start + depth, :].astype(BF16)
                for half in range(2):
                    dest = half * QUADS + quad
                    if batch == 0:
                        outs[0][dest, :FLAG_ROWS, :] = flags
                        outs[0][dest, FLAG_ROWS:, :] = value
                    else:
                        outs[batch][dest] = value


def stack_kernel(total_segs, first, own_ref, halo_ref, flag_ref, *refs):
    outs, scratch = refs[:-1], refs[-1]
    half, quad = lax.axis_index("h"), lax.axis_index("q")
    srcs, _, width = own_ref.shape
    depth = GROUP * 8

    def inverse(value):
        value = value.astype(F32)
        total = jnp.sum(value * value, axis=(0, 1))[None, :]
        return lax.rsqrt(total * (1.0 / (GROUP * total_segs)) + 1e-06)

    own_scale = inverse(own_ref[:, first : first + depth, :])
    col_scale = jnp.concatenate([own_scale, inverse(halo_ref[...])], axis=1) * (1.0 / total_segs)
    pick = lax.broadcasted_iota(jnp.int32, (64, width), 1) == (
        64 * half + 63 - lax.broadcasted_iota(jnp.int32, (64, width), 0)
    )
    row_scale = jnp.sum(jnp.where(pick, own_scale, 0.0), axis=1, keepdims=True)
    scale = row_scale * col_scale
    pick = pick.astype(F32).astype(BF16)

    row = lax.broadcasted_iota(jnp.int32, (depth, depth), 0)
    col = lax.broadcasted_iota(jnp.int32, (depth, depth), 1)
    flags = flag_ref[:, :FLAG_ROWS, :].reshape(depth, width).astype(F32)
    place = []
    for bin_ in range(2):
        keep = (col // 8) % 2 == bin_
        sign = jnp.where((col // 4) % 2 == 0, 1.0, -1.0)
        place.append(jnp.where(keep & (row == col), flags, 0.0))
        place.append(jnp.where(keep & (row == (col ^ 4)), flags * sign, 0.0))
    place = jnp.concatenate(place, axis=1).astype(BF16)

    owns = []
    for pair in range(GROUP // 2):
        rows = slice(first + 16 * pair, first + 16 * pair + 16)
        owns.append(own_ref[:, rows, :].reshape(depth, width))
    turned = dot_nt(pick, jnp.concatenate(owns, axis=0)).astype(BF16)
    turned = jnp.concatenate([turned[:, depth * k : depth * k + depth] for k in range(GROUP // 2)], axis=0)
    lefts = jnp.dot(turned, place, preferred_element_type=F32).astype(BF16)

    def fill(which):
        for pair in range(GROUP // 2):
            rows = slice(first + 16 * pair, first + 16 * pair + 16)
            behind = halo_ref[:, 16 * pair : 16 * pair + 16, :].reshape(depth, width)
            left = lefts[64 * pair : 64 * pair + 64]
            left = jnp.concatenate([left[:, 128 * k : 128 * k + 128] for k in range(4)], axis=0)
            right = jnp.concatenate([owns[pair], behind], axis=1)
            both = jnp.dot(left, right, preferred_element_type=F32)
            for bin_ in range(2):
                for part in range(2):
                    k = 2 * bin_ + part
                    block = both[64 * k : 64 * k + 64] * scale
                    block = pltpu.roll(block, 193 - 64 * which, 1, stride=1, stride_axis=0)
                    scratch[pl.ds(part * 16 + 2 * pair + bin_, 64, stride=32), :] = block[:, :OFFS]

    for which in range(2):
        pl.when(half == which)(functools.partial(fill, which))
    for slot in range(QUADS):
        if len(outs) == 1:
            outs[0][slot] = scratch[(3 - slot) * 512 : (4 - slot) * 512, :].astype(BF16)
        else:
            start = pl.multiple_of((3 - (quad ^ slot)) * 512, 512)
            outs[slot][...] = scratch[pl.ds(start, 512), :].astype(BF16)


def turn_kernel(*refs):
    parts, out_ref, scratch = refs[:-2], refs[-2], refs[-1]
    quad = lax.axis_index("q")
    count = out_ref.shape[0]
    sources = [(quad ^ slot, 0, ref) for slot, ref in enumerate(parts[:QUADS])]
    sources += [(source, 1, parts[QUADS].at[source]) for source in range(QUADS)]
    for source, batch, ref in sources:
        group = source * BATCHES + batch
        for row in range(count):
            for part in range(2):
                start = pl.multiple_of(part * 128 + GROUP * group, GROUP)
                begin = (2 * row + part) * GROUP
                scratch[count - 1 - row, pl.ds(start, GROUP), :] = ref[begin : begin + GROUP, :]
    eye = unit(OFFS)
    for row in range(count):
        out_ref[row] = dot_nt(eye, scratch[row]).astype(BF16)


def spectra(raw, alive, use):
    channels, segs, nsamp = raw.shape
    depth = 2 * BINS * segs // (QUADS * BATCHES)
    part = nsamp // N_STEPS
    return pl.pallas_call(
        functools.partial(spectrum_kernel, nsamp),
        out_shape=[
            jax.ShapeDtypeStruct((2 * QUADS, depth + (FLAG_ROWS if batch == 0 else 0), channels), BF16)
            for batch in range(BATCHES)
        ],
        grid=(N_STEPS,),
        in_specs=[
            SMEM,
            VMEM,
            pl.BlockSpec((channels, segs, part), lambda step: (0, 0, step)),
            pl.BlockSpec((part, 2 * BINS), lambda step: (step, 0)),
        ],
        out_specs=[VMEM] * BATCHES,
        scratch_shapes=[
            pltpu.VMEM((2, channels * segs + 8, BINS), F32),
            pltpu.VMEM((channels * segs, 128), F32),
            pltpu.VMEM((2 * BINS * segs + 8, channels), F32),
        ],
        compiler_params=BIG,
        name="spectra",
    )(use, alive[None, :], raw, basis_columns(nsamp))


def stack_pairs(own, halo, flags, total_segs, first):
    if first == 0:
        shapes = [jax.ShapeDtypeStruct((QUADS, 512, OFFS), BF16)]
    else:
        shapes = [jax.ShapeDtypeStruct((512, OFFS), BF16)] * QUADS
    return pl.pallas_call(
        functools.partial(stack_kernel, total_segs, first),
        out_shape=shapes,
        in_specs=[VMEM] * 3,
        out_specs=[VMEM] * len(shapes),
        scratch_shapes=[pltpu.VMEM((512 * QUADS + 32, OFFS), F32)],
        cost_estimate=pl.CostEstimate(flops=2 * 8 * 256 * 256 * 256 * 100, bytes_accessed=100 * 2**20, transcendentals=0),
        compiler_params=SMALL,
        name="stack",
    )(own, halo, flags)


def turn_pieces(pieces, sub):
    steps = 2
    return pl.pallas_call(
        turn_kernel,
        out_shape=jax.ShapeDtypeStruct((sub, OFFS, 2 * BINS), BF16),
        grid=(steps,),
        in_specs=[pl.BlockSpec((512 // steps, OFFS), lambda step: (steps - 1 - step, 0))] * QUADS
        + [pl.BlockSpec((QUADS, 512 // steps, OFFS), lambda step: (0, steps - 1 - step, 0))],
        out_specs=pl.BlockSpec((sub // steps, OFFS, 2 * BINS), lambda step: (step, 0, 0)),
        scratch_shapes=[pltpu.VMEM((sub // steps, 2 * BINS, OFFS), BF16)],
        compiler_params=SMALL,
        name="turn",
    )(*pieces)


def shards(raw, alive, use):
    channels, seg_local, _ = raw.shape
    chans = lax.axis_size("chan")
    total_segs = seg_local * lax.axis_size("h") * lax.axis_size("q")
    axes = ("chan", "h", "q")

    def index(chan, half, quad):
        return (chan * 2 + half) * QUADS + quad

    places = [(c, h, q) for c in range(chans) for h in range(2) for q in range(QUADS)]
    behind = [(index(c, h, q), index(c - 1, h if c % 2 else 1 - h, q)) for c, h, q in places if c > 0]

    owns = [lax.all_to_all(message, ("h", "q"), 0, 0, tiled=True) for message in spectra(raw, alive, use)]
    halos = [lax.ppermute(own[:, -GROUP * 8 :], axes, behind) for own in owns]
    pieces = []
    for batch, (own, halo) in enumerate(zip(owns, halos)):
        first = FLAG_ROWS if batch == 0 else 0
        stacked = stack_pairs(own, halo, owns[0], total_segs, first)
        if batch == 1:
            pieces.append(lax.all_to_all(stacked[0], "q", 0, 0, tiled=True))
            continue
        part = [stacked[0]] + [None] * (QUADS - 1)
        for slot in (1, 3, 2):
            pairs = [(index(c, h, q), index(c, h, q ^ slot)) for c, h, q in places]
            part[slot] = lax.ppermute(stacked[slot], axes, pairs)
        pieces += part
    return turn_pieces(pieces, channels // (2 * QUADS))


def solution(mesh):
    chans, groups = mesh.devices.shape
    fine = Mesh(mesh.devices.reshape(chans, 2, groups // 2), ("chan", "h", "q"))
    in_specs = (P("chan", ("h", "q"), None), P("chan"), P(("h", "q")))
    out_specs = P(("chan", "h", "q"), None, None)
    return jax.shard_map(shards, mesh=fine, in_specs=in_specs, out_specs=out_specs, check_vma=False)
```

```python
import functools
import math

import jax
import jax.numpy as jnp
import ml_dtypes
import numpy as np
from jax import lax
from jax.experimental import pallas as pl
from jax.experimental.pallas import tpu as pltpu
from jax.sharding import Mesh
from jax.sharding import PartitionSpec as P

BINS = 128
OFFS = 128
GROUP = 16
QUADS = 4
BATCHES = 2
FLAG_ROWS = 16
N_STEPS = 2
F32 = jnp.float32
BF16 = jnp.bfloat16
VMEM = pl.BlockSpec(memory_space=pltpu.VMEM)
SMEM = pl.BlockSpec(memory_space=pltpu.SMEM)
SMALL = pltpu.CompilerParams(vmem_limit_bytes=16 * 2**20)
BIG = pltpu.CompilerParams(vmem_limit_bytes=60 * 2**20)


def basis_columns(nsamp):
    times = np.arange(nsamp, dtype=np.int32)[:, None]
    freqs = np.arange(1, BINS + 1, dtype=np.int32)[None, :]
    phase = (times * freqs % nsamp).astype(np.float32) * np.float32(2.0 * math.pi / nsamp)
    scale = np.float32(1.0 / math.sqrt(nsamp))
    both = np.stack([np.cos(phase) * scale, -np.sin(phase) * scale], axis=-1)
    return both.reshape(nsamp, 2 * BINS).astype(ml_dtypes.bfloat16)


def dot_nt(left, right):
    return lax.dot_general(left, right, (((1,), (1,)), ((), ())), preferred_element_type=F32)


def unit(size):
    rows = lax.broadcasted_iota(jnp.int32, (size, size), 0)
    return (rows == lax.broadcasted_iota(jnp.int32, (size, size), 1)).astype(F32).astype(BF16)


def spectrum_kernel(nsamp, use_ref, alive_ref, raw_ref, basis_ref, *refs):
    outs, (spec, square, turned) = refs[:-3], refs[-3:]
    channels, segs, part = raw_ref.shape
    step = pl.program_id(0)
    flat = raw_ref[...].reshape(channels * segs, part)
    signal = flat.astype(F32)
    signal = signal * signal
    squares = signal[:, :128]
    for col in range(128, part, 128):
        squares += signal[:, col : col + 128]
    product = jnp.dot(flat, basis_ref[...], preferred_element_type=F32)

    @pl.when(step == 0)
    def _():
        for col in range(2):
            spec[col, : channels * segs] = product[:, 128 * col : 128 * col + 128]
        square[...] = squares

    @pl.when(step > 0)
    def _():
        for col in range(2):
            spec[col, : channels * segs] += product[:, 128 * col : 128 * col + 128]
        square[...] += squares

    @pl.when(step == pl.num_programs(0) - 1)
    def _():
        meansq = jnp.sum(square[...], axis=1, keepdims=True) * (1.0 / nsamp)
        scale = lax.rsqrt(meansq + 1e-06)
        for col in range(2):
            spec[col, : channels * segs] = jnp.where(scale > 0, spec[col, : channels * segs] * scale, 0.0)
        width = 2 * 128
        alive = alive_ref[...].astype(F32)
        for seg in range(segs):
            rows = [spec[col, pl.ds(seg, channels, stride=segs), :].astype(BF16) for col in range(2)]
            rows = jnp.concatenate(rows, axis=1)
            turned[pl.ds(seg, width, stride=segs), :] = dot_nt(unit(width), rows) * alive
        seg_of_row = lax.broadcasted_iota(jnp.int32, (FLAG_ROWS, channels), 0) % segs
        flags = jnp.zeros((FLAG_ROWS, channels), F32)
        for seg in range(segs):
            flags = jnp.where(seg_of_row == seg, use_ref[seg].astype(F32), flags)
        flags = flags.astype(BF16)
        depth = width * segs // (QUADS * BATCHES)
        for quad in range(QUADS):
            for batch in range(BATCHES):
                start = (quad * BATCHES + batch) * depth
                value = turned[start : start + depth, :].astype(BF16)
                for half in range(2):
                    dest = half * QUADS + quad
                    if batch == 0:
                        outs[0][dest, :FLAG_ROWS, :] = flags
                        outs[0][dest, FLAG_ROWS:, :] = value
                    else:
                        outs[batch][dest] = value


def stack_kernel(total_segs, first, own_ref, halo_ref, flag_ref, *refs):
    outs, scratch = refs[:-1], refs[-1]
    half, quad = lax.axis_index("h"), lax.axis_index("q")
    srcs, _, width = own_ref.shape
    depth = GROUP * 8

    def inverse(value):
        value = value.astype(F32)
        total = jnp.sum(value * value, axis=(0, 1))[None, :]
        return lax.rsqrt(total * (1.0 / (GROUP * total_segs)) + 1e-06)

    own_scale = inverse(own_ref[:, first : first + depth, :])
    col_scale = jnp.concatenate([own_scale, inverse(halo_ref[...])], axis=1) * (1.0 / total_segs)
    pick = lax.broadcasted_iota(jnp.int32, (64, width), 1) == (
        64 * half + 63 - lax.broadcasted_iota(jnp.int32, (64, width), 0)
    )
    row_scale = jnp.sum(jnp.where(pick, own_scale, 0.0), axis=1, keepdims=True)
    scale = row_scale * col_scale
    pick = pick.astype(F32).astype(BF16)

    row = lax.broadcasted_iota(jnp.int32, (depth, depth), 0)
    col = lax.broadcasted_iota(jnp.int32, (depth, depth), 1)
    flags = flag_ref[:, :FLAG_ROWS, :].reshape(depth, width).astype(F32)
    place = []
    for bin_ in range(2):
        keep = (col // 8) % 2 == bin_
        sign = jnp.where((col // 4) % 2 == 0, 1.0, -1.0)
        place.append(jnp.where(keep & (row == col), flags, 0.0))
        place.append(jnp.where(keep & (row == (col ^ 4)), flags * sign, 0.0))
    place = jnp.concatenate(place, axis=1).astype(BF16)

    owns = []
    for pair in range(GROUP // 2):
        rows = slice(first + 16 * pair, first + 16 * pair + 16)
        owns.append(own_ref[:, rows, :].reshape(depth, width))
    turned = dot_nt(pick, jnp.concatenate(owns, axis=0)).astype(BF16)
    turned = jnp.concatenate([turned[:, depth * k : depth * k + depth] for k in range(GROUP // 2)], axis=0)
    lefts = jnp.dot(turned, place, preferred_element_type=F32).astype(BF16)

    def fill(which):
        for pair in range(GROUP // 2):
            rows = slice(first + 16 * pair, first + 16 * pair + 16)
            behind = halo_ref[:, 16 * pair : 16 * pair + 16, :].reshape(depth, width)
            left = lefts[64 * pair : 64 * pair + 64]
            left = jnp.concatenate([left[:, 128 * k : 128 * k + 128] for k in range(4)], axis=0)
            right = jnp.concatenate([owns[pair], behind], axis=1)
            both = jnp.dot(left, right, preferred_element_type=F32)
            for bin_ in range(2):
                for part in range(2):
                    k = 2 * bin_ + part
                    block = both[64 * k : 64 * k + 64] * scale
                    block = pltpu.roll(block, 193 - 64 * which, 1, stride=1, stride_axis=0)
                    scratch[pl.ds(part * 16 + 2 * pair + bin_, 64, stride=32), :] = block[:, :OFFS]

    for which in range(2):
        pl.when(half == which)(functools.partial(fill, which))
    for slot in range(QUADS):
        if len(outs) == 1:
            outs[0][slot] = scratch[(3 - slot) * 512 : (4 - slot) * 512, :].astype(BF16)
        else:
            start = pl.multiple_of((3 - (quad ^ slot)) * 512, 512)
            outs[slot][...] = scratch[pl.ds(start, 512), :].astype(BF16)


def turn_kernel(*refs):
    parts, out_ref, scratch = refs[:-2], refs[-2], refs[-1]
    quad = lax.axis_index("q")
    count = out_ref.shape[0]
    sources = [(quad ^ slot, 0, ref) for slot, ref in enumerate(parts[:QUADS])]
    sources += [(source, 1, parts[QUADS].at[source]) for source in range(QUADS)]
    for source, batch, ref in sources:
        group = source * BATCHES + batch
        for row in range(count):
            for part in range(2):
                start = pl.multiple_of(part * 128 + GROUP * group, GROUP)
                begin = (2 * row + part) * GROUP
                scratch[count - 1 - row, pl.ds(start, GROUP), :] = ref[begin : begin + GROUP, :]
    eye = unit(OFFS)
    for row in range(count):
        out_ref[row] = dot_nt(eye, scratch[row]).astype(BF16)


def spectra(raw, alive, use):
    channels, segs, nsamp = raw.shape
    depth = 2 * BINS * segs // (QUADS * BATCHES)
    part = nsamp // N_STEPS
    return pl.pallas_call(
        functools.partial(spectrum_kernel, nsamp),
        out_shape=[
            jax.ShapeDtypeStruct((2 * QUADS, depth + (FLAG_ROWS if batch == 0 else 0), channels), BF16)
            for batch in range(BATCHES)
        ],
        grid=(N_STEPS,),
        in_specs=[
            SMEM,
            VMEM,
            pl.BlockSpec((channels, segs, part), lambda step: (0, 0, step)),
            pl.BlockSpec((part, 2 * BINS), lambda step: (step, 0)),
        ],
        out_specs=[VMEM] * BATCHES,
        scratch_shapes=[
            pltpu.VMEM((2, channels * segs + 8, BINS), F32),
            pltpu.VMEM((channels * segs, 128), F32),
            pltpu.VMEM((2 * BINS * segs + 8, channels), F32),
        ],
        compiler_params=BIG,
        name="spectra",
    )(use, alive[None, :], raw, basis_columns(nsamp))


def stack_pairs(own, halo, flags, total_segs, first):
    if first == 0:
        shapes = [jax.ShapeDtypeStruct((QUADS, 512, OFFS), BF16)]
    else:
        shapes = [jax.ShapeDtypeStruct((512, OFFS), BF16)] * QUADS
    return pl.pallas_call(
        functools.partial(stack_kernel, total_segs, first),
        out_shape=shapes,
        in_specs=[VMEM] * 3,
        out_specs=[VMEM] * len(shapes),
        scratch_shapes=[pltpu.VMEM((512 * QUADS + 32, OFFS), F32)],
        cost_estimate=pl.CostEstimate(flops=2 * 8 * 256 * 256 * 256 * 100, bytes_accessed=100 * 2**20, transcendentals=0),
        compiler_params=SMALL,
        name="stack",
    )(own, halo, flags)


def turn_pieces(pieces, sub):
    steps = 4
    return pl.pallas_call(
        turn_kernel,
        out_shape=jax.ShapeDtypeStruct((sub, OFFS, 2 * BINS), BF16),
        grid=(steps,),
        in_specs=[pl.BlockSpec((512 // steps, OFFS), lambda step: (steps - 1 - step, 0))] * QUADS
        + [pl.BlockSpec((QUADS, 512 // steps, OFFS), lambda step: (0, steps - 1 - step, 0))],
        out_specs=pl.BlockSpec((sub // steps, OFFS, 2 * BINS), lambda step: (step, 0, 0)),
        scratch_shapes=[pltpu.VMEM((sub // steps, 2 * BINS, OFFS), BF16)],
        compiler_params=SMALL,
        name="turn",
    )(*pieces)


def shards(raw, alive, use):
    channels, seg_local, _ = raw.shape
    chans = lax.axis_size("chan")
    total_segs = seg_local * lax.axis_size("h") * lax.axis_size("q")
    axes = ("chan", "h", "q")

    def index(chan, half, quad):
        return (chan * 2 + half) * QUADS + quad

    places = [(c, h, q) for c in range(chans) for h in range(2) for q in range(QUADS)]
    behind = [(index(c, h, q), index(c - 1, h if c % 2 else 1 - h, q)) for c, h, q in places if c > 0]

    owns = [lax.all_to_all(message, ("h", "q"), 0, 0, tiled=True) for message in spectra(raw, alive, use)]
    halos = [lax.ppermute(own[:, -GROUP * 8 :], axes, behind) for own in owns]
    pieces = []
    for batch, (own, halo) in enumerate(zip(owns, halos)):
        first = FLAG_ROWS if batch == 0 else 0
        stacked = stack_pairs(own, halo, owns[0], total_segs, first)
        if batch == 1:
            pieces.append(lax.all_to_all(stacked[0], "q", 0, 0, tiled=True))
            continue
        part = [stacked[0]] + [None] * (QUADS - 1)
        for slot in (1, 3, 2):
            pairs = [(index(c, h, q), index(c, h, q ^ slot)) for c, h, q in places]
            part[slot] = lax.ppermute(stacked[slot], axes, pairs)
        pieces += part
    return turn_pieces(pieces, channels // (2 * QUADS))


def solution(mesh):
    chans, groups = mesh.devices.shape
    fine = Mesh(mesh.devices.reshape(chans, 2, groups // 2), ("chan", "h", "q"))
    in_specs = (P("chan", ("h", "q"), None), P("chan"), P(("h", "q")))
    out_specs = P(("chan", "h", "q"), None, None)
    return jax.shard_map(shards, mesh=fine, in_specs=in_specs, out_specs=out_specs, check_vma=False)
```
